128 devices in a mesh: node: 16 (over y, x), local: 8 (over z, core).
Axes of the slice: x: 4, y: 4, z: 4, core: 2. Of those that a mesh axis runs over, the one named last changes fastest.
Arguments:
- tokens: bfloat16 [16384, 2048], P(('node', 'local')), may hold values from -6 to 6
- cotangent: bfloat16 [16384, 2048], P(('node', 'local')), may hold values from -6 to 6
- gates: bfloat16 [16384, 2], P(('node', 'local')), may hold values from 0.099609375 to 1
- expert_ids: int32 [16384, 2], P(('node', 'local')), may hold values from 0 to 127, as said below
- slots: int32 [16384, 2], P(('node', 'local')), may hold values from 0 to 3, as said below
- w_gate: bfloat16 [128, 2048, 1024], P(('node', 'local')), may hold values from -0.125 to 0.125
- w_up: bfloat16 [128, 2048, 1024], P(('node', 'local')), may hold values from -0.125 to 0.125
- w_down: bfloat16 [128, 1024, 2048], P(('node', 'local')), may hold values from -0.1875 to 0.1875
Outputs:
- grad_in: bfloat16 [16384, 2048], P(('node', 'local'))
- grad_gates: bfloat16 [16384, 2], P(('node', 'local'))
- grad_w_gate: bfloat16 [128, 2048, 1024], P(('node', 'local'))
- grad_w_up: bfloat16 [128, 2048, 1024], P(('node', 'local'))
- grad_w_down: bfloat16 [128, 1024, 2048], P(('node', 'local'))
The draws below stay inside these ranges and needn't reach their ends.
Inputs may be any that keep to these rules, and one draw needn't show every extreme that they name: `expert_ids`: each token names two different experts; among the 128 tokens of one device no expert is named more than 4 times, and one expert is named exactly 4 times by the tokens of every device; among the tokens of one device, the pairs naming the experts held by one node group number exactly 16. Within the tokens of one device, the pairs naming one expert take the slots 0 to their count minus 1, each once.
All inputs are finite; a program needn't handle non-finite values.
Results may differ from the reference program's by a relative error of at most 0.012.
Values may be sent and summed in bfloat16 or wider, within the bound.
A program may use at most 128 MiB of HBM per device.

```python
import jax
import jax.numpy as jnp
from jax import lax

D = 2048
H = 1024
TOK_DEV = 128
EXPERTS = 128
MOST = 4
TOKENS = 16384


def route_table(key):
    n_blocks = TOKENS // TOK_DEV
    half = MOST // 2
    pair_count = EXPERTS // 2
    chosen = jax.random.randint(jax.random.fold_in(key, 7), (), 0, pair_count).astype(jnp.int32)
    chosen_sign = (jax.random.randint(jax.random.fold_in(key, 9), (), 0, 2) * 2 - 1).astype(jnp.int32)

    def one_block(block):
        block_key = jax.random.fold_in(key, block + 11)
        key_delta, key_sign, key_order = jax.random.split(block_key, 3)
        delta = jax.random.randint(key_delta, (pair_count,), 0, half + 1).astype(jnp.int32)
        signs = (jax.random.randint(key_sign, (pair_count,), 0, 2) * 2 - 1).astype(jnp.int32)
        is_chosen = jnp.arange(pair_count, dtype=jnp.int32) == chosen
        delta = jnp.where(is_chosen, half, delta)
        signs = jnp.where(is_chosen, chosen_sign, signs)
        loads = jnp.stack([half + signs * delta, half - signs * delta], axis=1).reshape(-1)
        ends = jnp.cumsum(loads)
        starts = ends - loads
        entry = jnp.arange(2 * TOK_DEV, dtype=jnp.int32)
        expert = jnp.sum((entry[:, None] >= ends[None, :]).astype(jnp.int32), axis=1).astype(jnp.int32)
        slot = entry - starts[expert]
        token_order = jax.random.permutation(key_order, TOK_DEV).astype(jnp.int32)
        ids = jnp.zeros((TOK_DEV, 2), jnp.int32).at[token_order].set(jnp.stack([expert[:TOK_DEV], expert[TOK_DEV:]], axis=1))
        slot_table = jnp.zeros((TOK_DEV, 2), jnp.int32).at[token_order].set(jnp.stack([slot[:TOK_DEV], slot[TOK_DEV:]], axis=1))
        return (ids, slot_table)
    ids, slot_table = jax.vmap(one_block)(jnp.arange(n_blocks, dtype=jnp.int32))
    return (ids.reshape(TOKENS, 2), slot_table.reshape(TOKENS, 2))


def draw_expert_ids(key, part):
    return route_table(jax.random.fold_in(key, 3))[0]


def draw_slots(key, part):
    return route_table(jax.random.fold_in(key, 3))[1]


def block_scale(stream_key, shape, shards, least, largest):
    factor_of = 1.0
    for axis_at, blocks in shards:
        draws = jax.random.uniform(jax.random.fold_in(jax.random.fold_in(stream_key, 6), axis_at), (blocks,), jnp.float32, least / len(shards), largest / len(shards))
        factor_of = factor_of * jnp.repeat(jnp.exp(draws), shape[axis_at] // blocks).reshape((-1,) + (1,) * (len(shape) - 1 - axis_at))
    return factor_of


def noise(own_key, dims, deviation, bound, cuts=(), held_as=jnp.bfloat16):
    values = deviation * jax.random.normal(own_key, dims, jnp.float32)
    if cuts:
        values = values * block_scale(own_key, dims, cuts, -0.22, 0.18)
    return jnp.clip(values, -bound, bound).astype(held_as)


def setup_inputs(seed: int = 0) -> dict:
    splits = jax.random.split(jax.random.key(seed), 9)
    tokens = noise(splits[0], (TOKENS, D), 1.0, 6.0, ((0, 128),))
    cotangent = noise(splits[1], (TOKENS, D), 1.0, 6.0, ((0, 128),))
    gates = jnp.clip(0.099609375 + 0.9003906 * jax.random.uniform(splits[2], (TOKENS, 2), jnp.float32) ** block_scale(splits[2], (TOKENS, 2), ((0, 128),), -0.2, 0.2), 0.099609375, 1.0).astype(jnp.bfloat16)
    expert_ids = draw_expert_ids(jax.random.fold_in(splits[8], 71), 0)
    slots = draw_slots(jax.random.fold_in(splits[8], 71), 0)
    w_gate = noise(splits[5], (EXPERTS, D, H), D ** -0.5, 0.125, ((0, 128),))
    w_up = noise(splits[6], (EXPERTS, D, H), D ** -0.5, 0.125, ((0, 128),))
    w_down = noise(splits[7], (EXPERTS, H, D), H ** -0.5, 0.1875, ((0, 128),))
    return dict(tokens=tokens, cotangent=cotangent, gates=gates, expert_ids=expert_ids, slots=slots, w_gate=w_gate, w_up=w_up, w_down=w_down)


def expert_backward(rows_x, rows_dy, rows_gate, gate_w, up_w, down_w):
    gate_pre = jnp.dot(rows_x, gate_w, preferred_element_type=jnp.float32)
    up_pre = jnp.dot(rows_x, up_w, preferred_element_type=jnp.float32)
    sigmoid_gate = jax.nn.sigmoid(gate_pre)
    act = gate_pre * sigmoid_gate
    hidden = (act * up_pre).astype(jnp.bfloat16)
    expert_out = jnp.dot(hidden, down_w, preferred_element_type=jnp.float32)
    gate_term = jnp.sum(rows_dy.astype(jnp.float32) * expert_out, axis=-1).astype(jnp.bfloat16)
    scaled = (rows_gate.astype(jnp.float32)[:, None] * rows_dy.astype(jnp.float32)).astype(jnp.bfloat16)
    d_hidden = jnp.dot(scaled, down_w.T, preferred_element_type=jnp.float32)
    d_gate_pre = (d_hidden * up_pre * sigmoid_gate * (1.0 + gate_pre * (1.0 - sigmoid_gate))).astype(jnp.bfloat16)
    d_up_pre = (d_hidden * act).astype(jnp.bfloat16)
    row_grad = (jnp.dot(d_gate_pre, gate_w.T, preferred_element_type=jnp.float32)
                + jnp.dot(d_up_pre, up_w.T, preferred_element_type=jnp.float32)).astype(jnp.bfloat16)
    grad_gate_w = jnp.dot(rows_x.T, d_gate_pre, preferred_element_type=jnp.float32).astype(jnp.bfloat16)
    grad_up_w = jnp.dot(rows_x.T, d_up_pre, preferred_element_type=jnp.float32).astype(jnp.bfloat16)
    grad_down_w = jnp.dot(hidden.T, scaled, preferred_element_type=jnp.float32).astype(jnp.bfloat16)
    return row_grad, gate_term, grad_gate_w, grad_up_w, grad_down_w


def reference(tokens, cotangent, gates, expert_ids, slots, w_gate, w_up, w_down):
    n_blocks = TOKENS // TOK_DEV
    capacity = n_blocks * MOST
    token_index = jnp.arange(TOKENS, dtype=jnp.int32)
    source = (token_index // TOK_DEV)[:, None]
    position = (expert_ids * capacity + source * MOST + slots).astype(jnp.int32)
    entries = jnp.arange(2 * TOKENS, dtype=jnp.int32)
    table = jnp.full((EXPERTS * capacity,), 2 * TOKENS, dtype=jnp.int32)
    table = table.at[position.reshape(-1)].set(entries).reshape(EXPERTS, capacity)
    width = tokens.shape[1]
    tok_ext = jnp.concatenate([tokens, jnp.zeros((1, width), jnp.bfloat16)], axis=0)
    cot_ext = jnp.concatenate([cotangent, jnp.zeros((1, width), jnp.bfloat16)], axis=0)
    gate_ext = jnp.concatenate([gates.reshape(-1), jnp.zeros((1,), jnp.bfloat16)], axis=0)

    def one_expert(carry, inputs):
        accum, gate_flat = carry
        gate_w, up_w, down_w, index_row = inputs
        token_row = (index_row // 2).astype(jnp.int32)
        rows_x = jnp.take(tok_ext, token_row, axis=0)
        rows_dy = jnp.take(cot_ext, token_row, axis=0)
        rows_gate = jnp.take(gate_ext, index_row, axis=0)
        row_grad, gate_term, grad_gate_w, grad_up_w, grad_down_w = expert_backward(
            rows_x, rows_dy, rows_gate, gate_w, up_w, down_w)
        accum = accum.at[token_row].add(row_grad.astype(jnp.float32))
        gate_flat = gate_flat.at[index_row].set(gate_term)
        return (accum, gate_flat), (grad_gate_w, grad_up_w, grad_down_w)

    start = (jnp.zeros((TOKENS + 1, width), jnp.float32), jnp.zeros((2 * TOKENS + 1,), jnp.bfloat16))
    (accum, gate_flat), grads = lax.scan(one_expert, start, (w_gate, w_up, w_down, table))
    grad_in = accum[:TOKENS].astype(jnp.bfloat16)
    grad_gates = gate_flat[:2 * TOKENS].reshape(TOKENS, 2)
    return grad_in, grad_gates, grads[0], grads[1], grads[2]
```

```python
import functools

import jax
import jax.numpy as jnp
from jax import lax
from jax.experimental import pallas as pl
from jax.experimental.pallas import tpu as pltpu
from jax.sharding import PartitionSpec as P

MESH = pl.DeviceIdType.MESH
BF = jnp.bfloat16
F32 = jnp.float32
LANES = 128
NT = (((1,), (1,)), ((), ()))
TN = (((0,), (0,)), ((), ()))


def iota(shape, dim):
    return lax.broadcasted_iota(jnp.int32, shape, dim)


def layer_kernel(
    dims,
    ids_ref, slots_ref, gates_ref, tok_ref, cot_ref, wg_hbm, wu_hbm, wd_hbm,
    gin_ref, ggate_ref, xs_hbm, hid_hbm, dg_hbm, du_hbm,
    wg, wu, wd, gx, gs, bk, ms, mr, s1, r1, pk, s2, r2, hid, dg, du, s3, r3, s4, r4,
    w_sem, out_sem, n_send, n_recv, m_send, m_recv, z_send, z_recv, b_send, b_recv, h_send, h_recv,
):
    Y, X, L, RG, CAP, D, H = dims
    NG = Y * X
    NP = NG * RG
    TOK = tok_ref.shape[0]
    XC = X * CAP
    XR = X * RG
    ROWS = L * XC
    DR = D + LANES
    n = lax.axis_index("node")
    l = lax.axis_index("local")
    y = n // X
    x = lax.rem(n, X)

    def node_of(yy, xx):
        return lax.rem(yy + Y, Y) * X + lax.rem(xx + X, X)

    barrier = pltpu.get_barrier_semaphore()
    for k in range(Y):
        for dx in range(X):
            if k or dx:
                pl.semaphore_signal(
                    barrier, inc=1, device_id=(node_of(y + k, x + dx), l), device_id_type=MESH
                )
    for d in range(1, L):
        pl.semaphore_signal(barrier, inc=1, device_id=(n, lax.rem(l + d, L)), device_id_type=MESH)

    loads = [
        pltpu.make_async_copy(src.at[0], dst, w_sem.at[i])
        for i, (src, dst) in enumerate(((wg_hbm, wg), (wu_hbm, wu), (wd_hbm, wd)))
    ]
    for load in loads:
        load.start()

    e = ids_ref[...]
    s = slots_ref[...]
    gate = gates_ref[...].astype(F32)
    grp = e // L
    gi = iota((NG, TOK), 0)
    o0 = (grp[0:1] == gi).astype(F32)
    o1 = (grp[1:2] == gi).astype(F32)
    tri = (iota((TOK, TOK), 0) < iota((TOK, TOK), 1)).astype(F32).astype(BF)
    c0 = jnp.dot(o0.astype(BF), tri, preferred_element_type=F32)
    c1 = jnp.dot(o1.astype(BF), tri, preferred_element_type=F32)
    total0 = jnp.sum(o0, axis=1, keepdims=True)
    rank0 = jnp.sum(o0 * c0, axis=0, keepdims=True)
    rank1 = jnp.sum(o1 * (c1 + total0), axis=0, keepdims=True)
    pos0 = (grp[0:1] * RG).astype(F32) + rank0
    pos1 = (grp[1:2] * RG).astype(F32) + rank1
    pi = iota((NP, TOK), 0).astype(F32)
    b0 = (pi == pos0).astype(F32)
    b1 = (pi == pos1).astype(F32)
    gx[...] = (b0 + b1).astype(BF)
    gs[...] = (b0 * gate[0:1] + b1 * gate[1:2]).astype(BF)
    bk[0] = b0.astype(BF)
    bk[1] = b1.astype(BF)

    v = (e - grp * L) * XC + x * CAP + s
    v0 = jnp.broadcast_to(v[0:1], (8, TOK)).astype(F32).astype(BF)
    v1 = jnp.broadcast_to(v[1:2], (8, TOK)).astype(F32).astype(BF)
    val = lax.dot_general(v0, bk[0], NT, preferred_element_type=F32) + lax.dot_general(
        v1, bk[1], NT, preferred_element_type=F32
    )
    own = (iota((NG, NP), 1) // RG == iota((NG, NP), 0)).astype(F32)
    pp = iota((NP, LANES), 0)
    pick = (iota((NP, LANES), 1) == x * RG + lax.rem(pp, RG)).astype(F32).astype(BF)
    meta = jnp.dot((own * val[0:1]).astype(BF), pick, preferred_element_type=F32)
    for g in range(NG):
        ms[g] = jnp.broadcast_to(meta[g : g + 1], (8, LANES))

    def row_copy(k, dx):
        g = node_of(y - k, x + dx)
        return pltpu.make_async_remote_copy(
            s1.at[g], r1.at[k, x], n_send.at[k, dx], n_recv.at[k, dx],
            device_id=(g, l), device_id_type=MESH,
        )

    def meta_copy(k, dx):
        g = node_of(y - k, x + dx)
        return pltpu.make_async_remote_copy(
            ms.at[g], mr.at[k, x], m_send.at[k, dx], m_recv.at[k, dx],
            device_id=(g, l), device_id_type=MESH,
        )

    def row_arrival(k, dx):
        xs = lax.rem(x - dx + X, X)
        return pltpu.make_async_remote_copy(
            s1.at[n], r1.at[k, xs], n_send.at[k, dx], n_recv.at[k, dx],
            device_id=(node_of(y + k, xs), l), device_id_type=MESH,
        )

    def meta_arrival(k, dx):
        xs = lax.rem(x - dx + X, X)
        return pltpu.make_async_remote_copy(
            ms.at[n], mr.at[k, xs], m_send.at[k, dx], m_recv.at[k, dx],
            device_id=(node_of(y + k, xs), l), device_id_type=MESH,
        )

    def z_copy(k, d):
        j = lax.rem(l + d, L)
        return pltpu.make_async_remote_copy(
            s2.at[k, j], r2.at[k, l], z_send.at[k, d], z_recv.at[k, d],
            device_id=(n, j), device_id_type=MESH,
        )

    def z_arrival(k, d):
        j = lax.rem(l - d + L, L)
        return pltpu.make_async_remote_copy(
            s2.at[k, j], r2.at[k, j], z_send.at[k, d], z_recv.at[k, d],
            device_id=(n, j), device_id_type=MESH,
        )

    def b_copy(k, d):
        j = lax.rem(l + d, L)
        return pltpu.make_async_remote_copy(
            s3.at[k, j], r3.at[k, l], b_send.at[k, d], b_recv.at[k, d],
            device_id=(n, j), device_id_type=MESH,
        )

    def b_arrival(k, d):
        j = lax.rem(l - d + L, L)
        return pltpu.make_async_remote_copy(
            s3.at[k, j], r3.at[k, j], b_send.at[k, d], b_recv.at[k, d],
            device_id=(n, j), device_id_type=MESH,
        )

    def home_copy(k, dx):
        xs = lax.rem(x + dx, X)
        return pltpu.make_async_remote_copy(
            s4.at[k, xs], r4.at[n], h_send.at[k, dx], h_recv.at[k, dx],
            device_id=(node_of(y + k, xs), l), device_id_type=MESH,
        )

    def home_arrival(k, dx):
        g = node_of(y - k, x - dx)
        return pltpu.make_async_remote_copy(
            s4.at[k, x], r4.at[g], h_send.at[k, dx], h_recv.at[k, dx],
            device_id=(g, l), device_id_type=MESH,
        )

    def tiles(width, tile, body):
        def step(i, carry):
            body(pl.multiple_of(i * tile, tile))
            return carry

        lax.fori_loop(0, width // tile, step, 0)

    td = min(512, D)
    th = min(256, H)

    def node_send(k):
        yy = lax.rem(y - k + Y, Y)
        rows = pl.ds(pl.multiple_of(yy * XR, XR), XR)
        groups = pl.ds(yy * X, X)

        def body(c):
            a = jnp.dot(gx[rows, :], tok_ref[:, pl.ds(c, td)], preferred_element_type=F32)
            s1[groups, :, pl.ds(c, td)] = a.astype(BF).reshape(X, RG, td)
            b = jnp.dot(gs[rows, :], cot_ref[:, pl.ds(c, td)], preferred_element_type=F32)
            s1[groups, :, pl.ds(c + D, td)] = b.astype(BF).reshape(X, RG, td)

        tiles(D, td, body)
        if k == 0:
            pl.semaphore_wait(barrier, NG + L - 2)
        for dx in range(X):
            if k or dx:
                meta_copy(k, dx).start()
                row_copy(k, dx).start()
            else:
                r1[0, x] = s1[n]
                mr[0, x] = ms[n]

    def z_step(k):
        for dx in range(X):
            if k or dx:
                meta_arrival(k, dx).wait_recv()
                row_arrival(k, dx).wait_recv()
        target = mr[k, 0]
        for xs in range(1, X):
            target = target + mr[k, xs]
        place = iota((ROWS, XR), 0).astype(F32) == target[0:1, :XR]
        pk[k] = place.astype(F32)
        perm = place.astype(F32).astype(BF)

        def body(c):
            rows = r1[k, :, :, pl.ds(c, td)].reshape(XR, td)
            a = jnp.dot(perm, rows, preferred_element_type=F32)
            s2[k, :, :, pl.ds(c, td)] = a.astype(BF).reshape(L, XC, td)

        tiles(2 * D, td, body)
        for d in range(1, L):
            z_copy(k, d).start()
        r2[k, l] = s2[k, l]

    saves = []

    def compute(k):
        for d in range(1, L):
            z_arrival(k, d).wait_recv()
        if k == 0:
            for load in loads:
                load.wait()

        def fwd(i, u):
            c = pl.multiple_of(i * th, th)
            xr = r2[k, :, :, 0:D].reshape(ROWS, D)
            sr = r2[k, :, :, D : 2 * D].reshape(ROWS, D)
            gp = jnp.dot(xr, wg[:, pl.ds(c, th)], preferred_element_type=F32)
            up = jnp.dot(xr, wu[:, pl.ds(c, th)], preferred_element_type=F32)
            dh = lax.dot_general(sr, wd[pl.ds(c, th), :], NT, preferred_element_type=F32)
            sig = jax.nn.sigmoid(gp)
            act = gp * sig
            hf = act * up
            hid[k, :, pl.ds(c, th)] = hf.astype(BF)
            dg[k, :, pl.ds(c, th)] = (dh * up * sig * (1.0 + gp * (1.0 - sig))).astype(BF)
            du[k, :, pl.ds(c, th)] = (dh * act).astype(BF)
            return u + jnp.sum(hf * dh, axis=1, keepdims=True)

        u = lax.fori_loop(0, H // th, fwd, jnp.zeros((ROWS, 1), F32))

        def bwd(c):
            a = lax.dot_general(dg[k], wg[pl.ds(c, th), :], NT, preferred_element_type=F32)
            a = a + lax.dot_general(du[k], wu[pl.ds(c, th), :], NT, preferred_element_type=F32)
            s3[k, :, :, pl.ds(c, th)] = a.astype(BF).reshape(L, XC, th)

        tiles(D, th, bwd)
        hi = u.astype(BF).astype(F32)
        col = iota((ROWS, LANES), 1)
        both = jnp.where(col == 0, hi, jnp.where(col == 1, u - hi, 0.0))
        s3[k, :, :, D:DR] = both.astype(BF).reshape(L, XC, LANES)
        for i, (src, dst) in enumerate(((r2, xs_hbm), (hid, hid_hbm), (dg, dg_hbm), (du, du_hbm))):
            save = pltpu.make_async_copy(src.at[k], dst.at[k], out_sem.at[k, i])
            save.start()
            saves.append(save)

    def back_send(k):
        for d in range(1, L):
            b_copy(k, d).start()
        r3[k, l] = s3[k, l]

    def home_step(k):
        for d in range(1, L):
            b_arrival(k, d).wait_recv()
        perm = pk[k].T.astype(BF)
        t3 = DR // 17 if DR % 17 == 0 else LANES

        def body(c):
            rows = r3[k, :, :, pl.ds(c, td)].reshape(ROWS, td)
            a = jnp.dot(perm, rows, preferred_element_type=F32)
            s4[k, :, :, pl.ds(c, td)] = a.astype(BF).reshape(X, RG, td)

        tiles(D, td, body)
        a = jnp.dot(perm, r3[k, :, :, D:DR].reshape(ROWS, LANES), preferred_element_type=F32)
        s4[k, :, :, D:DR] = a.astype(BF).reshape(X, RG, LANES)
        for dx in range(X):
            if k or dx:
                home_copy(k, dx).start()
            else:
                r4[n] = s4[0, x]

    for k in range(Y):
        node_send(k)
    order = [("z", 0), ("z", 1)]
    for k in range(Y):
        order.append(("c", k))
        if k + 2 < Y:
            order.append(("z", k + 2))
    for what, k in order:
        if what == "z":
            z_step(k)
        else:
            compute(k)
            if k == Y - 1:
                pass
            back_send(k)
    for k in range(Y):
        home_step(k)

    for k in range(Y):
        for dx in range(X):
            if k or dx:
                home_arrival(k, dx).wait_recv()
    collect = gx[...].astype(F32).T.astype(BF)

    def body(c):
        rows = r4[:, :, pl.ds(c, td)].reshape(NP, td)
        gin_ref[:, pl.ds(c, td)] = jnp.dot(collect, rows, preferred_element_type=F32).astype(BF)

    tiles(D, td, body)
    sums = r4[:, :, D:DR].reshape(NP, LANES).astype(F32).T.astype(BF)
    for k in range(2):
        t = jnp.dot(sums, bk[k], preferred_element_type=F32)
        ggate_ref[k : k + 1, :] = ((t[0:1] + t[1:2]) / gate[k : k + 1]).astype(BF)

    for save in saves:
        save.wait()
    for k in range(Y):
        for dx in range(X):
            if k or dx:
                meta_copy(k, dx).wait_send()
                row_copy(k, dx).wait_send()
                home_copy(k, dx).wait_send()
        for d in range(1, L):
            z_copy(k, d).wait_send()
            b_copy(k, d).wait_send()


def weights_kernel(x_ref, sc_ref, hid_ref, dg_ref, du_ref, og_ref, ou_ref, od_ref):
    rows = x_ref.shape[0] * x_ref.shape[1]
    xt = x_ref[...].reshape(rows, -1)
    a = dg_ref[...].reshape(rows, -1)
    og_ref[0] = lax.dot_general(xt, a, TN, preferred_element_type=F32).astype(BF)
    b = du_ref[...].reshape(rows, -1)
    ou_ref[0] = lax.dot_general(xt, b, TN, preferred_element_type=F32).astype(BF)
    h = hid_ref[...].reshape(rows, -1)
    c = sc_ref[...].reshape(rows, -1)
    od_ref[0] = lax.dot_general(h, c, TN, preferred_element_type=F32).astype(BF)


def local(grid_y, tokens, cotangent, gates, expert_ids, slots, w_gate, w_up, w_down):
    tok, width = tokens.shape
    hidden = w_gate.shape[2]
    n_node = lax.axis_size("node")
    n_local = lax.axis_size("local")
    Y, X, L = grid_y, n_node // grid_y, n_local
    cap = 4 * tok // (n_node * n_local)
    RG = 2 * tok // n_node
    D, H = width, hidden
    XC, XR, ROWS, NP, DR = X * cap, X * RG, L * X * cap, 2 * tok, width + LANES
    vmem = pl.BlockSpec(memory_space=pltpu.VMEM)
    hbm = pl.BlockSpec(memory_space=pl.ANY)
    sem = pltpu.SemaphoreType.DMA
    shape = jax.ShapeDtypeStruct
    macs = 5 * Y * ROWS * D * H
    gin, ggate, xs, hid, dg, du = pl.pallas_call(
        functools.partial(layer_kernel, (Y, X, L, RG, cap, D, H)),
        out_shape=(
            shape((tok, D), BF),
            shape((2, tok), BF),
            shape((Y, L, XC, 2 * D), BF),
            shape((Y, ROWS, H), BF),
            shape((Y, ROWS, H), BF),
            shape((Y, ROWS, H), BF),
        ),
        in_specs=[vmem] * 5 + [hbm] * 3,
        out_specs=(vmem, vmem, hbm, hbm, hbm, hbm),
        scratch_shapes=[
            pltpu.VMEM((D, H), BF),
            pltpu.VMEM((D, H), BF),
            pltpu.VMEM((H, D), BF),
            pltpu.VMEM((NP, tok), BF),
            pltpu.VMEM((NP, tok), BF),
            pltpu.VMEM((2, NP, tok), BF),
            pltpu.VMEM((n_node, 8, LANES), F32),
            pltpu.VMEM((Y, X, 8, LANES), F32),
            pltpu.VMEM((n_node, RG, 2 * D), BF),
            pltpu.VMEM((Y, X, RG, 2 * D), BF),
            pltpu.VMEM((Y, ROWS, XR), F32),
            pltpu.VMEM((Y, L, XC, 2 * D), BF),
            pltpu.VMEM((Y, L, XC, 2 * D), BF),
            pltpu.VMEM((Y, ROWS, H), BF),
            pltpu.VMEM((Y, ROWS, H), BF),
            pltpu.VMEM((Y, ROWS, H), BF),
            pltpu.VMEM((Y, L, XC, DR), BF),
            pltpu.VMEM((Y, L, XC, DR), BF),
            pltpu.VMEM((Y, X, RG, DR), BF),
            pltpu.VMEM((n_node, RG, DR), BF),
            sem((3,)),
            sem((Y, 4)),
            sem((Y, X)),
            sem((Y, X)),
            sem((Y, X)),
            sem((Y, X)),
            sem((Y, L)),
            sem((Y, L)),
            sem((Y, L)),
            sem((Y, L)),
            sem((Y, X)),
            sem((Y, X)),
        ],
        compiler_params=pltpu.CompilerParams(
            collective_id=0, has_side_effects=True, vmem_limit_bytes=54 * 2**20
        ),
        cost_estimate=pl.CostEstimate(
            flops=2 * macs, bytes_accessed=24 * 2**20, transcendentals=Y * ROWS * H
        ),
        name="routed_layer",
    )(expert_ids.T, slots.T, gates.T, tokens, cotangent, w_gate, w_up, w_down)
    xs = xs.reshape(Y, ROWS, 2 * D)
    steps = 8
    bd, bh = D // steps, H // steps
    whole = lambda shape: pl.BlockSpec(shape, lambda i: (0, 0, 0))
    gg, gu, gd = pl.pallas_call(
        weights_kernel,
        grid=(steps,),
        out_shape=(shape((1, D, H), BF), shape((1, D, H), BF), shape((1, H, D), BF)),
        in_specs=[
            pl.BlockSpec((Y, ROWS, bd), lambda i: (0, 0, i)),
            pl.BlockSpec((Y, ROWS, D), lambda i: (0, 0, 1)),
            pl.BlockSpec((Y, ROWS, bh), lambda i: (0, 0, i)),
            whole((Y, ROWS, H)),
            whole((Y, ROWS, H)),
        ],
        out_specs=(
            pl.BlockSpec((1, bd, H), lambda i: (0, i, 0)),
            pl.BlockSpec((1, bd, H), lambda i: (0, i, 0)),
            pl.BlockSpec((1, bh, D), lambda i: (0, i, 0)),
        ),
        compiler_params=pltpu.CompilerParams(vmem_limit_bytes=48 * 2**20),
        cost_estimate=pl.CostEstimate(
            flops=6 * Y * ROWS * D * H, bytes_accessed=20 * 2**20, transcendentals=0
        ),
        name="weight_grads",
    )(xs, xs, hid, dg, du)
    return gin, ggate.T, gg, gu, gd


def solution(mesh):
    both = ("node", "local")
    n_node = mesh.shape["node"]
    grid_y = 1
    while (2 * grid_y) ** 2 <= n_node and n_node % (2 * grid_y) == 0:
        grid_y *= 2
    placed = (P(both, None),) * 5 + (P(both, None, None),) * 3
    return jax.shard_map(
        functools.partial(local, grid_y),
        mesh=mesh,
        in_specs=placed,
        out_specs=(P(both, None),) * 2 + (P(both, None, None),) * 3,
        check_vma=False,
    )
```

```python
import functools

import jax
import jax.numpy as jnp
from jax import lax
from jax.experimental import pallas as pl
from jax.experimental.pallas import tpu as pltpu
from jax.sharding import PartitionSpec as P

MESH = pl.DeviceIdType.MESH
BF = jnp.bfloat16
F32 = jnp.float32
LANES = 128
PLAN = (
    "t0", "n0", "n1", "n2", "n3", "z0", "f0", "z1", "g0", "z2", "c0", "z3", "b0", "k0", "c1",
    "b1", "k1", "c2", "k2", "w3", "b2", "c3", "b3", "k3", "h0", "h1", "h2", "h3",
)
NT = (((1,), (1,)), ((), ()))
TN = (((0,), (0,)), ((), ()))


def iota(shape, dim):
    return lax.broadcasted_iota(jnp.int32, shape, dim)


def layer_kernel(
    dims,
    ids_ref, slots_ref, gates_ref, tok_hbm, cot_hbm, wg_hbm, wu_hbm, wd_hbm,
    r4, bk, sc_hbm, xt_hbm, ht_hbm, dg_hbm, du_hbm,
    tok_ref, cot_ref, wg, wu, wd, gx, gs, ms, mr, s1, r1, pk, s2, r2, xt, ht, dg, du, s3, r3, s4,
    tb, ms2, mb, oh, sb, rb,
    w_sem, out_sem, n_send, n_recv, m_send, m_recv, z_send, z_recv, b_send, b_recv, h_send, h_recv,
    t_send, t_recv, f_send, f_recv, i_send, i_recv, g_send, g_recv,
):
    Y, X, L, RG, CAP, D, H = dims
    NG = Y * X
    NP = NG * RG
    TOK = tok_hbm.shape[0]
    XC = X * CAP
    XR = X * RG
    ROWS = L * XC
    DR = D + LANES
    BW = D // 2
    AW = 2 * D - BW
    Z = L // 2
    LC = L * CAP
    n = lax.axis_index("node")
    l = lax.axis_index("local")
    core = lax.rem(l, 2)
    zz = l // 2
    y = n // X
    x = lax.rem(n, X)
    offset = [0] + [o for i in range(1, Y // 2 + 1) for o in sorted({i, Y - i})]

    def node_of(yy, xx):
        return lax.rem(yy + Y, Y) * X + lax.rem(xx + X, X)

    barrier = pltpu.get_barrier_semaphore()
    for k in range(Y):
        for dx in range(X):
            if k or dx:
                pl.semaphore_signal(
                    barrier, inc=1, device_id=(node_of(y + k, x + dx), l), device_id_type=MESH
                )
    for d in range(1, L):
        pl.semaphore_signal(barrier, inc=1, device_id=(n, lax.rem(l + d, L)), device_id_type=MESH)

    loads = [
        pltpu.make_async_copy(src.at[0], dst, w_sem.at[i])
        for i, (src, dst) in enumerate(((wg_hbm, wg), (wu_hbm, wu), (wd_hbm, wd)))
    ]
    rows_in = [
        pltpu.make_async_copy(src, dst, w_sem.at[3 + i])
        for i, (src, dst) in enumerate(((tok_hbm, tok_ref), (cot_hbm, cot_ref)))
    ]
    for load in rows_in:
        load.start()
    for load in loads:
        load.start()

    e = ids_ref[...]
    s = slots_ref[...]
    gate = gates_ref[...].astype(F32)
    grp = e // L
    gi = iota((NG, TOK), 0)
    o0 = (grp[0:1] == gi).astype(F32)
    o1 = (grp[1:2] == gi).astype(F32)
    tri = (iota((TOK, TOK), 0) < iota((TOK, TOK), 1)).astype(F32).astype(BF)
    c0 = jnp.dot(o0.astype(BF), tri, preferred_element_type=F32)
    c1 = jnp.dot(o1.astype(BF), tri, preferred_element_type=F32)
    total0 = jnp.sum(o0, axis=1, keepdims=True)
    rank0 = jnp.sum(o0 * c0, axis=0, keepdims=True)
    rank1 = jnp.sum(o1 * (c1 + total0), axis=0, keepdims=True)
    pos0 = (grp[0:1] * RG).astype(F32) + rank0
    pos1 = (grp[1:2] * RG).astype(F32) + rank1
    pi = iota((NP, TOK), 0).astype(F32)
    b0 = (pi == pos0).astype(F32)
    b1 = (pi == pos1).astype(F32)
    gx[...] = (b0 + b1).astype(BF)
    gs[...] = (b0 * gate[0:1] + b1 * gate[1:2]).astype(BF)
    bk[0] = b0.astype(BF)
    bk[1] = b1.astype(BF)

    v = (e - grp * L) * XC + x * CAP + s
    v0 = jnp.broadcast_to(v[0:1], (8, TOK)).astype(F32).astype(BF)
    v1 = jnp.broadcast_to(v[1:2], (8, TOK)).astype(F32).astype(BF)
    val = lax.dot_general(v0, bk[0], NT, preferred_element_type=F32) + lax.dot_general(
        v1, bk[1], NT, preferred_element_type=F32
    )
    own = (iota((NG, NP), 1) // RG == iota((NG, NP), 0)).astype(F32)
    pp = iota((NP, LANES), 0)
    pick = (iota((NP, LANES), 1) == x * RG + lax.rem(pp, RG)).astype(F32).astype(BF)
    meta = jnp.dot((own * val[0:1]).astype(BF), pick, preferred_element_type=F32)
    for g in range(NG):
        ms[g] = jnp.broadcast_to(meta[g : g + 1], (8, LANES))

    def row_copy(k, dx):
        g = node_of(y - offset[k], x + dx)
        return pltpu.make_async_remote_copy(
            s1.at[g], r1.at[k, x], n_send.at[k, dx], n_recv.at[k, dx],
            device_id=(g, l), device_id_type=MESH,
        )

    def meta_copy(k, dx):
        g = node_of(y - offset[k], x + dx)
        return pltpu.make_async_remote_copy(
            ms.at[g], mr.at[k, x], m_send.at[k, dx], m_recv.at[k, dx],
            device_id=(g, l), device_id_type=MESH,
        )

    def row_arrival(k, dx):
        xs = lax.rem(x - dx + X, X)
        return pltpu.make_async_remote_copy(
            s1.at[n], r1.at[k, xs], n_send.at[k, dx], n_recv.at[k, dx],
            device_id=(node_of(y + offset[k], xs), l), device_id_type=MESH,
        )

    def meta_arrival(k, dx):
        xs = lax.rem(x - dx + X, X)
        return pltpu.make_async_remote_copy(
            ms.at[n], mr.at[k, xs], m_send.at[k, dx], m_recv.at[k, dx],
            device_id=(node_of(y + offset[k], xs), l), device_id_type=MESH,
        )

    def z_copy(k, d):
        j = lax.rem(l + d, L)
        return pltpu.make_async_remote_copy(
            s2.at[k, j], r2.at[k, l, :, pl.ds(BW, AW)], z_send.at[k, d], z_recv.at[k, d],
            device_id=(n, j), device_id_type=MESH,
        )

    def z_arrival(k, d):
        j = lax.rem(l - d + L, L)
        return pltpu.make_async_remote_copy(
            s2.at[k, j], r2.at[k, j, :, pl.ds(BW, AW)], z_send.at[k, d], z_recv.at[k, d],
            device_id=(n, j), device_id_type=MESH,
        )

    def b_copy(k, d):
        j = lax.rem(l + d, L)
        return pltpu.make_async_remote_copy(
            s3.at[k, j], r3.at[k, l], b_send.at[k, d], b_recv.at[k, d],
            device_id=(n, j), device_id_type=MESH,
        )

    def b_arrival(k, d):
        j = lax.rem(l - d + L, L)
        return pltpu.make_async_remote_copy(
            s3.at[k, j], r3.at[k, j], b_send.at[k, d], b_recv.at[k, d],
            device_id=(n, j), device_id_type=MESH,
        )

    def home_copy(k, dx):
        xs = lax.rem(x + dx, X)
        return pltpu.make_async_remote_copy(
            s4.at[k, xs], r4.at[n], h_send.at[k, dx], h_recv.at[k, dx],
            device_id=(node_of(y + offset[k], xs), l), device_id_type=MESH,
        )

    def home_arrival(k, dx):
        g = node_of(y - offset[k], x - dx)
        return pltpu.make_async_remote_copy(
            s4.at[k, x], r4.at[g], h_send.at[k, dx], h_recv.at[k, dx],
            device_id=(g, l), device_id_type=MESH,
        )

    def tiles(width, tile, body):
        def step(i, carry):
            body(pl.multiple_of(i * tile, tile))
            return carry

        lax.fori_loop(0, width // tile, step, 0)

    sent = []

    def send(copy):
        copy.start()
        sent.append(copy)

    td = min(512, BW)
    th = min(256, H)

    def t_copy(dz):
        j = lax.rem(zz + dz, Z) * 2 + core
        return pltpu.make_async_remote_copy(
            tb.at[l], tb.at[l], t_send.at[dz], t_recv.at[dz],
            device_id=(n, j), device_id_type=MESH,
        )

    def t_arrival(dz):
        j = lax.rem(zz - dz + Z, Z) * 2 + core
        return pltpu.make_async_remote_copy(
            tb.at[j], tb.at[j], t_send.at[dz], t_recv.at[dz],
            device_id=(n, j), device_id_type=MESH,
        )

    def f_copy(dz):
        j = lax.rem(zz - dz + Z, Z) * 2 + core
        return pltpu.make_async_remote_copy(
            tb.at[j], tb.at[j], f_send.at[dz], f_recv.at[dz],
            device_id=(n, l + 1 - 2 * core), device_id_type=MESH,
        )

    def f_arrival(dz):
        j = lax.rem(zz - dz + Z, Z) * 2 + 1 - core
        return pltpu.make_async_remote_copy(
            tb.at[j], tb.at[j], f_send.at[dz], f_recv.at[dz],
            device_id=(n, l + 1 - 2 * core), device_id_type=MESH,
        )

    def id_copy(d):
        j = lax.rem(l + d, L)
        return pltpu.make_async_remote_copy(
            ms2, mb.at[l], i_send.at[d], i_recv.at[d],
            device_id=(n, j), device_id_type=MESH,
        )

    def id_arrival(d):
        j = lax.rem(l - d + L, L)
        return pltpu.make_async_remote_copy(
            ms2, mb.at[j], i_send.at[d], i_recv.at[d],
            device_id=(n, j), device_id_type=MESH,
        )

    def g_copy(k, dx):
        g = node_of(y - offset[k], x + dx)
        return pltpu.make_async_remote_copy(
            sb.at[g], rb.at[n], g_send.at[k, dx], g_recv.at[k, dx],
            device_id=(g, l), device_id_type=MESH,
        )

    def g_arrival(k, dx):
        g = node_of(y + offset[k], x - dx)
        return pltpu.make_async_remote_copy(
            sb.at[n], rb.at[g], g_send.at[k, dx], g_recv.at[k, dx],
            device_id=(g, l), device_id_type=MESH,
        )

    def token_send(_):
        for load in rows_in:
            load.wait()
        tb[l] = tok_ref[:, 0:BW]
        ms2[...] = jnp.concatenate([e, s, e, s], axis=0).astype(F32)
        mb[l] = ms2[...]
        pl.semaphore_wait(barrier, NG + L - 2)
        for d in range(1, L):
            send(id_copy(d))
        for dz in range(1, Z):
            send(t_copy(dz))
        send(f_copy(0))

    def token_forward(_):
        for dz in range(1, Z):
            t_arrival(dz).wait_recv()
            send(f_copy(dz))

    def token_route(_):
        for d in range(1, L):
            id_arrival(d).wait_recv()
        row = iota((NG * LC, TOK), 0).astype(F32)
        for j in range(L):
            m = mb[j].astype(jnp.int32)
            ej, sj = m[0:2], m[2:4]
            gj = ej // L
            place = jnp.where(ej - gj * L == l, gj * LC + j * CAP + sj, -1).astype(F32)
            hit = (row == place[0:1]) | (row == place[1:2])
            oh[:, j * TOK : (j + 1) * TOK] = hit.astype(F32).astype(BF)
        for dz in range(Z):
            f_arrival(dz).wait_recv()

        def body(c):
            rows = tb[:, :, pl.ds(c, th)].reshape(L * TOK, th)
            a = jnp.dot(oh[...], rows, preferred_element_type=F32)
            sb[:, :, pl.ds(c, th)] = a.astype(BF).reshape(NG, LC, th)

        tiles(BW, th, body)
        for k in range(Y):
            for dx in range(X):
                if k or dx:
                    send(g_copy(k, dx))
        rb[n] = sb[n]

    def token_take(k):
        for dx in range(X):
            if k or dx:
                g_arrival(k, dx).wait_recv()
        out, col = iota((ROWS, ROWS), 0), iota((ROWS, ROWS), 1)
        src = lax.rem(out, XC) // CAP * LC + out // XC * CAP + lax.rem(out, CAP)
        perm = (src == col).astype(F32).astype(BF)
        nodes = pl.ds(lax.rem(y + offset[k], Y) * X, X)

        def body(c):
            rows = rb[nodes, :, pl.ds(c, td)].reshape(ROWS, td)
            a = jnp.dot(perm, rows, preferred_element_type=F32)
            r2[k, :, :, pl.ds(c, td)] = a.astype(BF).reshape(L, XC, td)

        tiles(BW, td, body)

    def node_send(k):
        yy = lax.rem(y - offset[k] + Y, Y)
        rows = pl.ds(pl.multiple_of(yy * XR, XR), XR)
        groups = pl.ds(yy * X, X)

        def own_x(c):
            a = jnp.dot(gx[rows, :], tok_ref[:, pl.ds(c + BW, td)], preferred_element_type=F32)
            s1[groups, :, pl.ds(c, td)] = a.astype(BF).reshape(X, RG, td)

        def own_scaled(c):
            b = jnp.dot(gs[rows, :], cot_ref[:, pl.ds(c, td)], preferred_element_type=F32)
            s1[groups, :, pl.ds(c + D - BW, td)] = b.astype(BF).reshape(X, RG, td)

        tiles(D - BW, td, own_x)
        tiles(D, td, own_scaled)
        for dx in range(X):
            if k or dx:
                send(meta_copy(k, dx))
                send(row_copy(k, dx))
            else:
                r1[0, x] = s1[n]
                mr[0, x] = ms[n]

    def z_step(k):
        for dx in range(X):
            if k or dx:
                meta_arrival(k, dx).wait_recv()
                row_arrival(k, dx).wait_recv()
        target = mr[k, 0]
        for xs in range(1, X):
            target = target + mr[k, xs]
        place = iota((ROWS, XR), 0).astype(F32) == target[0:1, :XR]
        pk[k] = place.astype(F32)
        perm = place.astype(F32).astype(BF)

        def body(c):
            rows = r1[k, :, :, pl.ds(c, td)].reshape(XR, td)
            a = jnp.dot(perm, rows, preferred_element_type=F32)
            s2[k, :, :, pl.ds(c, td)] = a.astype(BF).reshape(L, XC, td)

        tiles(AW, td, body)
        for d in range(1, L):
            send(z_copy(k, d))
        r2[k, l, :, BW:] = s2[k, l]

    saves = []

    arrived = set()

    def z_wait(k):
        if k not in arrived:
            arrived.add(k)
            for d in range(1, L):
                z_arrival(k, d).wait_recv()

    def compute(k):
        token_take(k)
        z_wait(k)
        if k == 0:
            for load in loads:
                load.wait()

        def fwd(i, u):
            c = pl.multiple_of(i * th, th)
            xr = r2[k, :, :, 0:D].reshape(ROWS, D)
            sr = r2[k, :, :, D : 2 * D].reshape(ROWS, D)
            gp = jnp.dot(xr, wg[:, pl.ds(c, th)], preferred_element_type=F32)
            up = jnp.dot(xr, wu[:, pl.ds(c, th)], preferred_element_type=F32)
            dh = lax.dot_general(sr, wd[pl.ds(c, th), :], NT, preferred_element_type=F32)
            sig = jax.nn.sigmoid(gp)
            act = gp * sig
            hf = act * up
            ht[pl.ds(c, th), k * ROWS : (k + 1) * ROWS] = hf.T.astype(BF)
            dg[k, :, pl.ds(c, th)] = (dh * up * sig * (1.0 + gp * (1.0 - sig))).astype(BF)
            du[k, :, pl.ds(c, th)] = (dh * act).astype(BF)
            return u + jnp.sum(hf * dh, axis=1, keepdims=True)

        u = lax.fori_loop(0, H // th, fwd, jnp.zeros((ROWS, 1), F32))

        def bwd(c):
            a = lax.dot_general(dg[k], wg[pl.ds(c, th), :], NT, preferred_element_type=F32)
            a = a + lax.dot_general(du[k], wu[pl.ds(c, th), :], NT, preferred_element_type=F32)
            s3[k, :, :, pl.ds(c, th)] = a.astype(BF).reshape(L, XC, th)

        tiles(D, th, bwd)
        hi = u.astype(BF).astype(F32)
        col = iota((ROWS, LANES), 1)
        both = jnp.where(col == 0, hi, jnp.where(col == 1, u - hi, 0.0))
        s3[k, :, :, D:DR] = both.astype(BF).reshape(L, XC, LANES)
        for i, (src, dst) in enumerate(((dg, dg_hbm), (du, du_hbm))):
            save = pltpu.make_async_copy(src.at[k], dst.at[k], out_sem.at[k, i])
            save.start()
            saves.append(save)

    def keep(k):
        def body(c):
            rows = r2[k, :, :, pl.ds(c, th)].reshape(ROWS, th)
            xt[pl.ds(c, th), k * ROWS : (k + 1) * ROWS] = rows.astype(F32).T.astype(BF)

        tiles(D, th, body)
        lanes = pl.ds(k * ROWS, ROWS)
        for i, (src, dst) in enumerate(
            (
                (r2.at[k, :, :, pl.ds(D, D)], sc_hbm.at[k]),
                (xt.at[:, lanes], xt_hbm.at[:, lanes]),
                (ht.at[:, lanes], ht_hbm.at[:, lanes]),
            )
        ):
            save = pltpu.make_async_copy(src, dst, out_sem.at[k, 2 + i])
            save.start()
            saves.append(save)

    def back_send(k):
        for d in range(1, L):
            send(b_copy(k, d))
        r3[k, l] = s3[k, l]

    def home_step(k):
        for d in range(1, L):
            b_arrival(k, d).wait_recv()
        perm = pk[k].T.astype(BF)

        def body(c):
            rows = r3[k, :, :, pl.ds(c, td)].reshape(ROWS, td)
            a = jnp.dot(perm, rows, preferred_element_type=F32)
            s4[k, :, :, pl.ds(c, td)] = a.astype(BF).reshape(X, RG, td)

        tiles(D, td, body)
        a = jnp.dot(perm, r3[k, :, :, D:DR].reshape(ROWS, LANES), preferred_element_type=F32)
        s4[k, :, :, D:DR] = a.astype(BF).reshape(X, RG, LANES)
        for dx in range(X):
            if k or dx:
                send(home_copy(k, dx))
            else:
                own_home.start()

    own_home = pltpu.make_async_copy(s4.at[0, x], r4.at[n], w_sem.at[5])
    phases = dict(t=token_send, f=token_forward, g=token_route, n=node_send, z=z_step, w=z_wait, c=compute, b=back_send, k=keep, h=home_step)
    for phase in PLAN:
        phases[phase[0]](int(phase[1]))

    for k in range(Y):
        for dx in range(X):
            if k or dx:
                home_arrival(k, dx).wait_recv()
    own_home.wait()
    for save in saves:
        save.wait()
    for copy in sent:
        copy.wait_send()


def outputs_kernel(
    tile,
    xt_hbm, sc_hbm, ht_hbm, dg_hbm, du_hbm, home_hbm, bk_ref, gate_ref,
    og_hbm, ou_hbm, od_hbm, gin_hbm, ggate_ref,
    xt, sc, ht, dg, du, home, og, ou, od, gin, in_sem, out_sem,
):
    D, H = xt.shape[0], ht.shape[0]
    parts = 4
    depth = D // parts
    pending = []

    def load(i, src, dst):
        copy = pltpu.make_async_copy(src, dst, in_sem.at[i])
        copy.start()
        return copy

    dg_load = load(0, dg_hbm, dg)
    xt_loads = [
        load(1 + i, xt_hbm.at[pl.ds(i * depth, depth)], xt.at[pl.ds(i * depth, depth)])
        for i in range(parts)
    ]
    du_load = load(parts + 1, du_hbm, du)
    ht_load = load(parts + 2, ht_hbm, ht)
    sc_load = load(parts + 3, sc_hbm, sc)
    home_load = load(parts + 4, home_hbm, home)

    def save(src, dst):
        copy = pltpu.make_async_copy(src, dst, out_sem.at[len(pending)])
        copy.start()
        pending.append(copy)

    def product(left, right, out, dst, waits):
        height = left.shape[0]
        for i, r in enumerate(range(0, height, tile)):
            if r in waits:
                waits[r].wait()
            rows = pl.ds(r, tile)
            right_rows = right[...].reshape(-1, right.shape[-1])
            a = jnp.dot(left[rows, :], right_rows, preferred_element_type=F32)
            out[rows, :] = a.astype(BF)
            save(out.at[rows], dst.at[0, rows])

    dg_load.wait()
    product(xt, dg, og, og_hbm, {i * depth: copy for i, copy in enumerate(xt_loads)})
    du_load.wait()
    product(xt, du, ou, ou_hbm, {})
    ht_load.wait()
    sc_load.wait()
    product(ht, sc, od, od_hbm, {})

    home_load.wait()
    both = (bk_ref[0].astype(F32) + bk_ref[1].astype(F32)).T.astype(BF)
    back = home[...].reshape(-1, home.shape[-1])
    gin[...] = jnp.dot(both, back[:, :D], preferred_element_type=F32).astype(BF)
    save(gin, gin_hbm)
    gate = gate_ref[...].astype(F32)
    sums = back[:, D:].astype(F32).T.astype(BF)
    for k in range(2):
        t = jnp.dot(sums, bk_ref[k], preferred_element_type=F32)
        ggate_ref[k : k + 1, :] = ((t[0:1] + t[1:2]) / gate[k : k + 1]).astype(BF)
    for copy in pending:
        copy.wait()


def local(grid_y, tokens, cotangent, gates, expert_ids, slots, w_gate, w_up, w_down):
    tok, width = tokens.shape
    hidden = w_gate.shape[2]
    n_node = lax.axis_size("node")
    n_local = lax.axis_size("local")
    Y, X, L = grid_y, n_node // grid_y, n_local
    cap = 4 * tok // (n_node * n_local)
    RG = 2 * tok // n_node
    D, H = width, hidden
    XC, XR, ROWS, NP, DR = X * cap, X * RG, L * X * cap, 2 * tok, width + LANES
    vmem = pl.BlockSpec(memory_space=pltpu.VMEM)
    hbm = pl.BlockSpec(memory_space=pl.ANY)
    sem = pltpu.SemaphoreType.DMA
    shape = jax.ShapeDtypeStruct
    macs = 5 * Y * ROWS * D * H
    home, bk, sc, xt, ht, dg, du = pl.pallas_call(
        functools.partial(layer_kernel, (Y, X, L, RG, cap, D, H)),
        out_shape=(
            shape((n_node, RG, DR), BF),
            shape((2, NP, tok), BF),
            shape((Y, L, XC, D), BF),
            shape((D, Y * ROWS), BF),
            shape((H, Y * ROWS), BF),
            shape((Y, ROWS, H), BF),
            shape((Y, ROWS, H), BF),
        ),
        in_specs=[vmem] * 3 + [hbm] * 5,
        out_specs=(hbm, vmem, hbm, hbm, hbm, hbm, hbm),
        scratch_shapes=[
            pltpu.VMEM((tok, D), BF),
            pltpu.VMEM((tok, D), BF),
            pltpu.VMEM((D, H), BF),
            pltpu.VMEM((D, H), BF),
            pltpu.VMEM((H, D), BF),
            pltpu.VMEM((NP, tok), BF),
            pltpu.VMEM((NP, tok), BF),
            pltpu.VMEM((n_node, 8, LANES), F32),
            pltpu.VMEM((Y, X, 8, LANES), F32),
            pltpu.VMEM((n_node, RG, 3 * D // 2), BF),
            pltpu.VMEM((Y, X, RG, 3 * D // 2), BF),
            pltpu.VMEM((Y, ROWS, XR), F32),
            pltpu.VMEM((Y, L, XC, 3 * D // 2), BF),
            pltpu.VMEM((Y, L, XC, 2 * D), BF),
            pltpu.VMEM((D, Y * ROWS), BF),
            pltpu.VMEM((H, Y * ROWS), BF),
            pltpu.VMEM((Y, ROWS, H), BF),
            pltpu.VMEM((Y, ROWS, H), BF),
            pltpu.VMEM((Y, L, XC, DR), BF),
            pltpu.VMEM((Y, L, XC, DR), BF),
            pltpu.VMEM((Y, X, RG, DR), BF),
            pltpu.VMEM((L, tok, D // 2), BF),
            pltpu.VMEM((8, tok), F32),
            pltpu.VMEM((L, 8, tok), F32),
            pltpu.VMEM((n_node * L * cap, L * tok), BF),
            pltpu.VMEM((n_node, L * cap, D // 2), BF),
            pltpu.VMEM((n_node, L * cap, D // 2), BF),
            sem((6,)),
            sem((Y, 5)),
            sem((Y, X)),
            sem((Y, X)),
            sem((Y, X)),
            sem((Y, X)),
            sem((Y, L)),
            sem((Y, L)),
            sem((Y, L)),
            sem((Y, L)),
            sem((Y, X)),
            sem((Y, X)),
            sem((L // 2,)),
            sem((L // 2,)),
            sem((L // 2,)),
            sem((L // 2,)),
            sem((L,)),
            sem((L,)),
            sem((Y, X)),
            sem((Y, X)),
        ],
        compiler_params=pltpu.CompilerParams(
            collective_id=0, has_side_effects=True, vmem_limit_bytes=54 * 2**20
        ),
        cost_estimate=pl.CostEstimate(
            flops=2 * macs, bytes_accessed=24 * 2**20, transcendentals=Y * ROWS * H
        ),
        name="routed_layer",
    )(expert_ids.T, slots.T, gates.T, tokens, cotangent, w_gate, w_up, w_down)
    sc = sc.reshape(Y, ROWS, D)
    tile = min(256, H)
    gg, gu, gd, gin, ggate = pl.pallas_call(
        functools.partial(outputs_kernel, tile),
        out_shape=(
            shape((1, D, H), BF),
            shape((1, D, H), BF),
            shape((1, H, D), BF),
            shape((tok, D), BF),
            shape((2, tok), BF),
        ),
        in_specs=[hbm] * 6 + [vmem] * 2,
        out_specs=(hbm, hbm, hbm, hbm, vmem),
        scratch_shapes=[
            pltpu.VMEM((D, Y * ROWS), BF),
            pltpu.VMEM((Y, ROWS, D), BF),
            pltpu.VMEM((H, Y * ROWS), BF),
            pltpu.VMEM((Y, ROWS, H), BF),
            pltpu.VMEM((Y, ROWS, H), BF),
            pltpu.VMEM((n_node, RG, DR), BF),
            pltpu.VMEM((D, H), BF),
            pltpu.VMEM((D, H), BF),
            pltpu.VMEM((H, D), BF),
            pltpu.VMEM((tok, D), BF),
            sem((9,)),
            sem(((2 * D + H) // tile + 1,)),
        ],
        compiler_params=pltpu.CompilerParams(vmem_limit_bytes=60 * 2**20),
        cost_estimate=pl.CostEstimate(
            flops=6 * Y * ROWS * D * H, bytes_accessed=20 * 2**20, transcendentals=0
        ),
        name="weight_grads",
    )(xt, sc, ht, dg, du, home, bk, gates.T)
    return gin, ggate.T, gg, gu, gd


def solution(mesh):
    both = ("node", "local")
    n_node = mesh.shape["node"]
    grid_y = 1
    while (2 * grid_y) ** 2 <= n_node and n_node % (2 * grid_y) == 0:
        grid_y *= 2
    placed = (P(both, None),) * 5 + (P(both, None, None),) * 3
    return jax.shard_map(
        functools.partial(local, grid_y),
        mesh=mesh,
        in_specs=placed,
        out_specs=(P(both, None),) * 2 + (P(both, None, None),) * 3,
        check_vma=False,
    )
```

```python
import functools

import jax
import jax.numpy as jnp
from jax import lax
from jax.experimental import pallas as pl
from jax.experimental.pallas import tpu as pltpu
from jax.sharding import PartitionSpec as P

MESH = pl.DeviceIdType.MESH
BF = jnp.bfloat16
F32 = jnp.float32
LANES = 128
PLAN = (
    "t0", "n0", "n1", "n2", "n3", "z0", "f0", "z1", "g0", "z2", "c0", "z3", "b0", "c1", "b1",
    "k0", "c2", "k1", "w3", "b2", "c3", "b3", "h0", "k2", "h1", "k3", "h2", "h3",
)
NT = (((1,), (1,)), ((), ()))
TN = (((0,), (0,)), ((), ()))


def iota(shape, dim):
    return lax.broadcasted_iota(jnp.int32, shape, dim)


def layer_kernel(
    dims,
    ids_ref, slots_ref, gates_ref, tok_hbm, cot_hbm, wg_hbm, wu_hbm, wd_hbm,
    r4, bk, sc_hbm, xt_hbm, ht_hbm, dg_hbm, du_hbm,
    tok_ref, cot_ref, wg, wu, wd, gx, gs, ms, mr, s1, r1, pk, s2, r2, xt, ht, dg, du, s3, r3, s4,
    tb, ms2, mb, oh, sb, rb,
    w_sem, out_sem, n_send, n_recv, m_send, m_recv, z_send, z_recv, b_send, b_recv, h_send, h_recv,
    t_send, t_recv, f_send, f_recv, i_send, i_recv, g_send, g_recv,
):
    Y, X, L, RG, CAP, D, H = dims
    NG = Y * X
    NP = NG * RG
    TOK = tok_hbm.shape[0]
    XC = X * CAP
    XR = X * RG
    ROWS = L * XC
    DR = D + LANES
    BW = D // 2
    AW = 2 * D - BW
    Z = L // 2
    LC = L * CAP
    n = lax.axis_index("node")
    l = lax.axis_index("local")
    core = lax.rem(l, 2)
    zz = l // 2
    y = n // X
    x = lax.rem(n, X)
    offset = [0] + [o for i in range(1, Y // 2 + 1) for o in sorted({i, Y - i})]

    def node_of(yy, xx):
        return lax.rem(yy + Y, Y) * X + lax.rem(xx + X, X)

    barrier = pltpu.get_barrier_semaphore()
    for k in range(Y):
        for dx in range(X):
            if k or dx:
                pl.semaphore_signal(
                    barrier, inc=1, device_id=(node_of(y + k, x + dx), l), device_id_type=MESH
                )
    for d in range(1, L):
        pl.semaphore_signal(barrier, inc=1, device_id=(n, lax.rem(l + d, L)), device_id_type=MESH)

    loads = [
        pltpu.make_async_copy(src.at[0], dst, w_sem.at[i])
        for i, (src, dst) in enumerate(((wg_hbm, wg), (wu_hbm, wu), (wd_hbm, wd)))
    ]
    rows_in = [
        pltpu.make_async_copy(src, dst, w_sem.at[3 + i])
        for i, (src, dst) in enumerate(((tok_hbm, tok_ref), (cot_hbm, cot_ref)))
    ]
    for load in rows_in:
        load.start()
    for load in loads:
        load.start()

    e = ids_ref[...]
    s = slots_ref[...]
    gate = gates_ref[...].astype(F32)
    grp = e // L
    gi = iota((NG, TOK), 0)
    o0 = (grp[0:1] == gi).astype(F32)
    o1 = (grp[1:2] == gi).astype(F32)
    tri = (iota((TOK, TOK), 0) < iota((TOK, TOK), 1)).astype(F32).astype(BF)
    c0 = jnp.dot(o0.astype(BF), tri, preferred_element_type=F32)
    c1 = jnp.dot(o1.astype(BF), tri, preferred_element_type=F32)
    total0 = jnp.sum(o0, axis=1, keepdims=True)
    rank0 = jnp.sum(o0 * c0, axis=0, keepdims=True)
    rank1 = jnp.sum(o1 * (c1 + total0), axis=0, keepdims=True)
    pos0 = (grp[0:1] * RG).astype(F32) + rank0
    pos1 = (grp[1:2] * RG).astype(F32) + rank1
    pi = iota((NP, TOK), 0).astype(F32)
    b0 = (pi == pos0).astype(F32)
    b1 = (pi == pos1).astype(F32)
    gx[...] = (b0 + b1).astype(BF)
    gs[...] = (b0 * gate[0:1] + b1 * gate[1:2]).astype(BF)
    bk[0] = b0.astype(BF)
    bk[1] = b1.astype(BF)

    v = (e - grp * L) * XC + x * CAP + s
    v0 = jnp.broadcast_to(v[0:1], (8, TOK)).astype(F32).astype(BF)
    v1 = jnp.broadcast_to(v[1:2], (8, TOK)).astype(F32).astype(BF)
    val = lax.dot_general(v0, bk[0], NT, preferred_element_type=F32) + lax.dot_general(
        v1, bk[1], NT, preferred_element_type=F32
    )
    own = (iota((NG, NP), 1) // RG == iota((NG, NP), 0)).astype(F32)
    pp = iota((NP, LANES), 0)
    pick = (iota((NP, LANES), 1) == x * RG + lax.rem(pp, RG)).astype(F32).astype(BF)
    meta = jnp.dot((own * val[0:1]).astype(BF), pick, preferred_element_type=F32)
    for g in range(NG):
        ms[g] = jnp.broadcast_to(meta[g : g + 1], (8, LANES))

    def row_copy(k, dx):
        g = node_of(y - offset[k], x + dx)
        return pltpu.make_async_remote_copy(
            s1.at[g], r1.at[k, x], n_send.at[k, dx], n_recv.at[k, dx],
            device_id=(g, l), device_id_type=MESH,
        )

    def meta_copy(k, dx):
        g = node_of(y - offset[k], x + dx)
        return pltpu.make_async_remote_copy(
            ms.at[g], mr.at[k, x], m_send.at[k, dx], m_recv.at[k, dx],
            device_id=(g, l), device_id_type=MESH,
        )

    def row_arrival(k, dx):
        xs = lax.rem(x - dx + X, X)
        return pltpu.make_async_remote_copy(
            s1.at[n], r1.at[k, xs], n_send.at[k, dx], n_recv.at[k, dx],
            device_id=(node_of(y + offset[k], xs), l), device_id_type=MESH,
        )

    def meta_arrival(k, dx):
        xs = lax.rem(x - dx + X, X)
        return pltpu.make_async_remote_copy(
            ms.at[n], mr.at[k, xs], m_send.at[k, dx], m_recv.at[k, dx],
            device_id=(node_of(y + offset[k], xs), l), device_id_type=MESH,
        )

    def z_copy(k, d):
        j = lax.rem(l + d, L)
        return pltpu.make_async_remote_copy(
            s2.at[k, j], r2.at[k, l, :, pl.ds(BW, AW)], z_send.at[k, d], z_recv.at[k, d],
            device_id=(n, j), device_id_type=MESH,
        )

    def z_arrival(k, d):
        j = lax.rem(l - d + L, L)
        return pltpu.make_async_remote_copy(
            s2.at[k, j], r2.at[k, j, :, pl.ds(BW, AW)], z_send.at[k, d], z_recv.at[k, d],
            device_id=(n, j), device_id_type=MESH,
        )

    def b_copy(k, d):
        j = lax.rem(l + d, L)
        return pltpu.make_async_remote_copy(
            s3.at[k, j], r3.at[k, l], b_send.at[k, d], b_recv.at[k, d],
            device_id=(n, j), device_id_type=MESH,
        )

    def b_arrival(k, d):
        j = lax.rem(l - d + L, L)
        return pltpu.make_async_remote_copy(
            s3.at[k, j], r3.at[k, j], b_send.at[k, d], b_recv.at[k, d],
            device_id=(n, j), device_id_type=MESH,
        )

    def home_copy(k, dx):
        xs = lax.rem(x + dx, X)
        return pltpu.make_async_remote_copy(
            s4.at[k, xs], r4.at[n], h_send.at[k, dx], h_recv.at[k, dx],
            device_id=(node_of(y + offset[k], xs), l), device_id_type=MESH,
        )

    def home_arrival(k, dx):
        g = node_of(y - offset[k], x - dx)
        return pltpu.make_async_remote_copy(
            s4.at[k, x], r4.at[g], h_send.at[k, dx], h_recv.at[k, dx],
            device_id=(g, l), device_id_type=MESH,
        )

    def tiles(width, tile, body):
        def step(i, carry):
            body(pl.multiple_of(i * tile, tile))
            return carry

        lax.fori_loop(0, width // tile, step, 0)

    sent = []

    def send(copy):
        copy.start()
        sent.append(copy)

    td = min(512, BW)
    th = min(256, H)

    def t_copy(dz):
        j = lax.rem(zz + dz, Z) * 2 + core
        return pltpu.make_async_remote_copy(
            tb.at[l], tb.at[l], t_send.at[dz], t_recv.at[dz],
            device_id=(n, j), device_id_type=MESH,
        )

    def t_arrival(dz):
        j = lax.rem(zz - dz + Z, Z) * 2 + core
        return pltpu.make_async_remote_copy(
            tb.at[j], tb.at[j], t_send.at[dz], t_recv.at[dz],
            device_id=(n, j), device_id_type=MESH,
        )

    def f_copy(dz):
        j = lax.rem(zz - dz + Z, Z) * 2 + core
        return pltpu.make_async_remote_copy(
            tb.at[j], tb.at[j], f_send.at[dz], f_recv.at[dz],
            device_id=(n, l + 1 - 2 * core), device_id_type=MESH,
        )

    def f_arrival(dz):
        j = lax.rem(zz - dz + Z, Z) * 2 + 1 - core
        return pltpu.make_async_remote_copy(
            tb.at[j], tb.at[j], f_send.at[dz], f_recv.at[dz],
            device_id=(n, l + 1 - 2 * core), device_id_type=MESH,
        )

    def id_copy(d):
        j = lax.rem(l + d, L)
        return pltpu.make_async_remote_copy(
            ms2, mb.at[l], i_send.at[d], i_recv.at[d],
            device_id=(n, j), device_id_type=MESH,
        )

    def id_arrival(d):
        j = lax.rem(l - d + L, L)
        return pltpu.make_async_remote_copy(
            ms2, mb.at[j], i_send.at[d], i_recv.at[d],
            device_id=(n, j), device_id_type=MESH,
        )

    def g_copy(k, dx):
        g = node_of(y - offset[k], x + dx)
        return pltpu.make_async_remote_copy(
            sb.at[g], rb.at[n], g_send.at[k, dx], g_recv.at[k, dx],
            device_id=(g, l), device_id_type=MESH,
        )

    def g_arrival(k, dx):
        g = node_of(y + offset[k], x - dx)
        return pltpu.make_async_remote_copy(
            sb.at[n], rb.at[g], g_send.at[k, dx], g_recv.at[k, dx],
            device_id=(g, l), device_id_type=MESH,
        )

    def token_send(_):
        for load in rows_in:
            load.wait()
        tb[l] = tok_ref[:, 0:BW]
        ms2[...] = jnp.concatenate([e, s, e, s], axis=0).astype(F32)
        mb[l] = ms2[...]
        pl.semaphore_wait(barrier, NG + L - 2)
        for d in range(1, L):
            send(id_copy(d))
        for dz in range(1, Z):
            send(t_copy(dz))
        send(f_copy(0))

    def token_forward(_):
        for dz in range(1, Z):
            t_arrival(dz).wait_recv()
            send(f_copy(dz))

    def token_route(_):
        for d in range(1, L):
            id_arrival(d).wait_recv()
        row = iota((NG * LC, TOK), 0).astype(F32)
        for j in range(L):
            m = mb[j].astype(jnp.int32)
            ej, sj = m[0:2], m[2:4]
            gj = ej // L
            place = jnp.where(ej - gj * L == l, gj * LC + j * CAP + sj, -1).astype(F32)
            hit = (row == place[0:1]) | (row == place[1:2])
            oh[:, j * TOK : (j + 1) * TOK] = hit.astype(F32).astype(BF)
        for dz in range(Z):
            f_arrival(dz).wait_recv()

        def body(c):
            rows = tb[:, :, pl.ds(c, th)].reshape(L * TOK, th)
            a = jnp.dot(oh[...], rows, preferred_element_type=F32)
            sb[:, :, pl.ds(c, th)] = a.astype(BF).reshape(NG, LC, th)

        tiles(BW, th, body)
        for k in range(Y):
            for dx in range(X):
                if k or dx:
                    send(g_copy(k, dx))
        rb[n] = sb[n]

    def token_take(k):
        for dx in range(X):
            if k or dx:
                g_arrival(k, dx).wait_recv()
        out, col = iota((ROWS, ROWS), 0), iota((ROWS, ROWS), 1)
        src = lax.rem(out, XC) // CAP * LC + out // XC * CAP + lax.rem(out, CAP)
        perm = (src == col).astype(F32).astype(BF)
        nodes = pl.ds(lax.rem(y + offset[k], Y) * X, X)

        def body(c):
            rows = rb[nodes, :, pl.ds(c, td)].reshape(ROWS, td)
            a = jnp.dot(perm, rows, preferred_element_type=F32)
            r2[k, :, :, pl.ds(c, td)] = a.astype(BF).reshape(L, XC, td)

        tiles(BW, td, body)

    def node_send(k):
        yy = lax.rem(y - offset[k] + Y, Y)
        rows = pl.ds(pl.multiple_of(yy * XR, XR), XR)
        groups = pl.ds(yy * X, X)

        def own_x(c):
            a = jnp.dot(gx[rows, :], tok_ref[:, pl.ds(c + BW, td)], preferred_element_type=F32)
            s1[groups, :, pl.ds(c, td)] = a.astype(BF).reshape(X, RG, td)

        def own_scaled(c):
            b = jnp.dot(gs[rows, :], cot_ref[:, pl.ds(c, td)], preferred_element_type=F32)
            s1[groups, :, pl.ds(c + D - BW, td)] = b.astype(BF).reshape(X, RG, td)

        tiles(D - BW, td, own_x)
        tiles(D, td, own_scaled)
        for dx in range(X):
            if k or dx:
                send(meta_copy(k, dx))
                send(row_copy(k, dx))
            else:
                r1[0, x] = s1[n]
                mr[0, x] = ms[n]

    def z_step(k):
        for dx in range(X):
            if k or dx:
                meta_arrival(k, dx).wait_recv()
                row_arrival(k, dx).wait_recv()
        target = mr[k, 0]
        for xs in range(1, X):
            target = target + mr[k, xs]
        place = iota((ROWS, XR), 0).astype(F32) == target[0:1, :XR]
        pk[k] = place.astype(F32)
        perm = place.astype(F32).astype(BF)

        def body(c):
            rows = r1[k, :, :, pl.ds(c, td)].reshape(XR, td)
            a = jnp.dot(perm, rows, preferred_element_type=F32)
            s2[k, :, :, pl.ds(c, td)] = a.astype(BF).reshape(L, XC, td)

        tiles(AW, td, body)
        for d in range(1, L):
            send(z_copy(k, d))
        r2[k, l, :, BW:] = s2[k, l]

    saves = []

    arrived = set()

    def z_wait(k):
        if k not in arrived:
            arrived.add(k)
            for d in range(1, L):
                z_arrival(k, d).wait_recv()

    def compute(k):
        token_take(k)
        z_wait(k)
        if k == 0:
            for load in loads:
                load.wait()

        def fwd(i, u):
            c = pl.multiple_of(i * th, th)
            xr = r2[k, :, :, 0:D].reshape(ROWS, D)
            sr = r2[k, :, :, D : 2 * D].reshape(ROWS, D)
            gp = jnp.dot(xr, wg[:, pl.ds(c, th)], preferred_element_type=F32)
            up = jnp.dot(xr, wu[:, pl.ds(c, th)], preferred_element_type=F32)
            dh = lax.dot_general(sr, wd[pl.ds(c, th), :], NT, preferred_element_type=F32)
            sig = jax.nn.sigmoid(gp)
            act = gp * sig
            hf = act * up
            ht[pl.ds(c, th), k * ROWS : (k + 1) * ROWS] = hf.T.astype(BF)
            dg[k, :, pl.ds(c, th)] = (dh * up * sig * (1.0 + gp * (1.0 - sig))).astype(BF)
            du[k, :, pl.ds(c, th)] = (dh * act).astype(BF)
            return u + jnp.sum(hf * dh, axis=1, keepdims=True)

        u = lax.fori_loop(0, H // th, fwd, jnp.zeros((ROWS, 1), F32))

        def bwd(c):
            a = lax.dot_general(dg[k], wg[pl.ds(c, th), :], NT, preferred_element_type=F32)
            a = a + lax.dot_general(du[k], wu[pl.ds(c, th), :], NT, preferred_element_type=F32)
            s3[k, :, :, pl.ds(c, th)] = a.astype(BF).reshape(L, XC, th)

        tiles(D, th, bwd)
        hi = u.astype(BF).astype(F32)
        col = iota((ROWS, LANES), 1)
        both = jnp.where(col == 0, hi, jnp.where(col == 1, u - hi, 0.0))
        s3[k, :, :, D:DR] = both.astype(BF).reshape(L, XC, LANES)
        for i, (src, dst) in enumerate(((dg, dg_hbm), (du, du_hbm))):
            save = pltpu.make_async_copy(src.at[k], dst.at[k], out_sem.at[k, i])
            save.start()
            saves.append(save)

    def keep(k):
        def body(c):
            rows = r2[k, :, :, pl.ds(c, th)].reshape(ROWS, th)
            xt[pl.ds(c, th), k * ROWS : (k + 1) * ROWS] = rows.astype(F32).T.astype(BF)

        tiles(D, th, body)
        lanes = pl.ds(k * ROWS, ROWS)
        for i, (src, dst) in enumerate(
            (
                (r2.at[k, :, :, pl.ds(D, D)], sc_hbm.at[k]),
                (xt.at[:, lanes], xt_hbm.at[:, lanes]),
                (ht.at[:, lanes], ht_hbm.at[:, lanes]),
            )
        ):
            save = pltpu.make_async_copy(src, dst, out_sem.at[k, 2 + i])
            save.start()
            saves.append(save)

    def back_send(k):
        for d in range(1, L):
            send(b_copy(k, d))
        r3[k, l] = s3[k, l]

    def home_step(k):
        for d in range(1, L):
            b_arrival(k, d).wait_recv()
        perm = pk[k].T.astype(BF)

        def body(c):
            rows = r3[k, :, :, pl.ds(c, td)].reshape(ROWS, td)
            a = jnp.dot(perm, rows, preferred_element_type=F32)
            s4[k, :, :, pl.ds(c, td)] = a.astype(BF).reshape(X, RG, td)

        tiles(D, td, body)
        a = jnp.dot(perm, r3[k, :, :, D:DR].reshape(ROWS, LANES), preferred_element_type=F32)
        s4[k, :, :, D:DR] = a.astype(BF).reshape(X, RG, LANES)
        for dx in range(X):
            if k or dx:
                send(home_copy(k, dx))
            else:
                own_home.start()

    own_home = pltpu.make_async_copy(s4.at[0, x], r4.at[n], w_sem.at[5])
    phases = dict(t=token_send, f=token_forward, g=token_route, n=node_send, z=z_step, w=z_wait, c=compute, b=back_send, k=keep, h=home_step)
    for phase in PLAN:
        phases[phase[0]](int(phase[1]))

    for k in range(Y):
        for dx in range(X):
            if k or dx:
                home_arrival(k, dx).wait_recv()
    own_home.wait()
    for save in saves:
        save.wait()
    for copy in sent:
        copy.wait_send()


def outputs_kernel(
    tile,
    xt_hbm, sc_hbm, ht_hbm, dg_hbm, du_hbm, home_hbm, bk_ref, gate_ref,
    og_hbm, ou_hbm, od_hbm, gin_hbm, ggate_ref,
    xt, sc, ht, dg, du, home, og, ou, od, gin, in_sem, out_sem,
):
    D, H = xt.shape[0], ht.shape[0]
    parts = 4
    depth = D // parts
    pending = []

    def load(i, src, dst):
        copy = pltpu.make_async_copy(src, dst, in_sem.at[i])
        copy.start()
        return copy

    dg_load = load(0, dg_hbm, dg)
    xt_loads = [
        load(1 + i, xt_hbm.at[pl.ds(i * depth, depth)], xt.at[pl.ds(i * depth, depth)])
        for i in range(parts)
    ]
    du_load = load(parts + 1, du_hbm, du)
    ht_load = load(parts + 2, ht_hbm, ht)
    sc_load = load(parts + 3, sc_hbm, sc)
    home_load = load(parts + 4, home_hbm, home)

    def save(src, dst):
        copy = pltpu.make_async_copy(src, dst, out_sem.at[len(pending)])
        copy.start()
        pending.append(copy)

    def product(left, right, out, dst, waits):
        height = left.shape[0]
        for i, r in enumerate(range(0, height, tile)):
            if r in waits:
                waits[r].wait()
            rows = pl.ds(r, tile)
            right_rows = right[...].reshape(-1, right.shape[-1])
            a = jnp.dot(left[rows, :], right_rows, preferred_element_type=F32)
            out[rows, :] = a.astype(BF)
            save(out.at[rows], dst.at[0, rows])

    dg_load.wait()
    product(xt, dg, og, og_hbm, {i * depth: copy for i, copy in enumerate(xt_loads)})
    du_load.wait()
    product(xt, du, ou, ou_hbm, {})
    ht_load.wait()
    sc_load.wait()
    product(ht, sc, od, od_hbm, {})

    home_load.wait()
    both = (bk_ref[0].astype(F32) + bk_ref[1].astype(F32)).T.astype(BF)
    back = home[...].reshape(-1, home.shape[-1])
    gin[...] = jnp.dot(both, back[:, :D], preferred_element_type=F32).astype(BF)
    save(gin, gin_hbm)
    gate = gate_ref[...].astype(F32)
    sums = back[:, D:].astype(F32).T.astype(BF)
    for k in range(2):
        t = jnp.dot(sums, bk_ref[k], preferred_element_type=F32)
        ggate_ref[k : k + 1, :] = ((t[0:1] + t[1:2]) / gate[k : k + 1]).astype(BF)
    for copy in pending:
        copy.wait()


def local(grid_y, tokens, cotangent, gates, expert_ids, slots, w_gate, w_up, w_down):
    tok, width = tokens.shape
    hidden = w_gate.shape[2]
    n_node = lax.axis_size("node")
    n_local = lax.axis_size("local")
    Y, X, L = grid_y, n_node // grid_y, n_local
    cap = 4 * tok // (n_node * n_local)
    RG = 2 * tok // n_node
    D, H = width, hidden
    XC, XR, ROWS, NP, DR = X * cap, X * RG, L * X * cap, 2 * tok, width + LANES
    vmem = pl.BlockSpec(memory_space=pltpu.VMEM)
    hbm = pl.BlockSpec(memory_space=pl.ANY)
    sem = pltpu.SemaphoreType.DMA
    shape = jax.ShapeDtypeStruct
    macs = 5 * Y * ROWS * D * H
    home, bk, sc, xt, ht, dg, du = pl.pallas_call(
        functools.partial(layer_kernel, (Y, X, L, RG, cap, D, H)),
        out_shape=(
            shape((n_node, RG, DR), BF),
            shape((2, NP, tok), BF),
            shape((Y, L, XC, D), BF),
            shape((D, Y * ROWS), BF),
            shape((H, Y * ROWS), BF),
            shape((Y, ROWS, H), BF),
            shape((Y, ROWS, H), BF),
        ),
        in_specs=[vmem] * 3 + [hbm] * 5,
        out_specs=(hbm, vmem, hbm, hbm, hbm, hbm, hbm),
        scratch_shapes=[
            pltpu.VMEM((tok, D), BF),
            pltpu.VMEM((tok, D), BF),
            pltpu.VMEM((D, H), BF),
            pltpu.VMEM((D, H), BF),
            pltpu.VMEM((H, D), BF),
            pltpu.VMEM((NP, tok), BF),
            pltpu.VMEM((NP, tok), BF),
            pltpu.VMEM((n_node, 8, LANES), F32),
            pltpu.VMEM((Y, X, 8, LANES), F32),
            pltpu.VMEM((n_node, RG, 3 * D // 2), BF),
            pltpu.VMEM((Y, X, RG, 3 * D // 2), BF),
            pltpu.VMEM((Y, ROWS, XR), F32),
            pltpu.VMEM((Y, L, XC, 3 * D // 2), BF),
            pltpu.VMEM((Y, L, XC, 2 * D), BF),
            pltpu.VMEM((D, Y * ROWS), BF),
            pltpu.VMEM((H, Y * ROWS), BF),
            pltpu.VMEM((Y, ROWS, H), BF),
            pltpu.VMEM((Y, ROWS, H), BF),
            pltpu.VMEM((Y, L, XC, DR), BF),
            pltpu.VMEM((Y, L, XC, DR), BF),
            pltpu.VMEM((Y, X, RG, DR), BF),
            pltpu.VMEM((L, tok, D // 2), BF),
            pltpu.VMEM((8, tok), F32),
            pltpu.VMEM((L, 8, tok), F32),
            pltpu.VMEM((n_node * L * cap, L * tok), BF),
            pltpu.VMEM((n_node, L * cap, D // 2), BF),
            pltpu.VMEM((n_node, L * cap, D // 2), BF),
            sem((6,)),
            sem((Y, 5)),
            sem((Y, X)),
            sem((Y, X)),
            sem((Y, X)),
            sem((Y, X)),
            sem((Y, L)),
            sem((Y, L)),
            sem((Y, L)),
            sem((Y, L)),
            sem((Y, X)),
            sem((Y, X)),
            sem((L // 2,)),
            sem((L // 2,)),
            sem((L // 2,)),
            sem((L // 2,)),
            sem((L,)),
            sem((L,)),
            sem((Y, X)),
            sem((Y, X)),
        ],
        compiler_params=pltpu.CompilerParams(
            collective_id=0, has_side_effects=True, vmem_limit_bytes=54 * 2**20
        ),
        cost_estimate=pl.CostEstimate(
            flops=2 * macs, bytes_accessed=24 * 2**20, transcendentals=Y * ROWS * H
        ),
        name="routed_layer",
    )(expert_ids.T, slots.T, gates.T, tokens, cotangent, w_gate, w_up, w_down)
    sc = sc.reshape(Y, ROWS, D)
    tile = min(256, H)
    gg, gu, gd, gin, ggate = pl.pallas_call(
        functools.partial(outputs_kernel, tile),
        out_shape=(
            shape((1, D, H), BF),
            shape((1, D, H), BF),
            shape((1, H, D), BF),
            shape((tok, D), BF),
            shape((2, tok), BF),
        ),
        in_specs=[hbm] * 6 + [vmem] * 2,
        out_specs=(hbm, hbm, hbm, hbm, vmem),
        scratch_shapes=[
            pltpu.VMEM((D, Y * ROWS), BF),
            pltpu.VMEM((Y, ROWS, D), BF),
            pltpu.VMEM((H, Y * ROWS), BF),
            pltpu.VMEM((Y, ROWS, H), BF),
            pltpu.VMEM((Y, ROWS, H), BF),
            pltpu.VMEM((n_node, RG, DR), BF),
            pltpu.VMEM((D, H), BF),
            pltpu.VMEM((D, H), BF),
            pltpu.VMEM((H, D), BF),
            pltpu.VMEM((tok, D), BF),
            sem((9,)),
            sem(((2 * D + H) // tile + 1,)),
        ],
        compiler_params=pltpu.CompilerParams(vmem_limit_bytes=60 * 2**20),
        cost_estimate=pl.CostEstimate(
            flops=6 * Y * ROWS * D * H, bytes_accessed=20 * 2**20, transcendentals=0
        ),
        name="weight_grads",
    )(xt, sc, ht, dg, du, home, bk, gates.T)
    return gin, ggate.T, gg, gu, gd


def solution(mesh):
    both = ("node", "local")
    n_node = mesh.shape["node"]
    grid_y = 1
    while (2 * grid_y) ** 2 <= n_node and n_node % (2 * grid_y) == 0:
        grid_y *= 2
    placed = (P(both, None),) * 5 + (P(both, None, None),) * 3
    return jax.shard_map(
        functools.partial(local, grid_y),
        mesh=mesh,
        in_specs=placed,
        out_specs=(P(both, None),) * 2 + (P(both, None, None),) * 3,
        check_vma=False,
    )
```
